32 devices in a mesh: groups: 2 (over y), ctx: 4 (over x, core), head: 4 (over z).
Axes of the slice: x: 2, y: 2, z: 4, core: 2. Of those that a mesh axis runs over, the one named last changes fastest.
Arguments:
- context: bfloat16 [8192, 1024], P(('groups', 'ctx', 'head')), parts along dimension 0, may hold values from -6 to 6
- w_kv: bfloat16 [1024, 2048], replicated, may hold values from -0.1875 to 0.1875
- queries: bfloat16 [32, 64, 2048], P(('groups', 'head')), parts along dimension 0, may hold values from -400 to 400
- gain: float32 [1024], replicated, may hold values from 0.25 to 1.75
- w_out: bfloat16 [1024, 1024], P('head'), may hold values from -0.1875 to 0.1875
Outputs:
- latent_out: bfloat16 [4096, 1024], P(('groups', 'ctx', 'head')), parts along dimension 0
The draws below stay inside these ranges and needn't reach their ends.
There are 2 independent parts, one for each index of `groups`. The reference program is written for one: setup_inputs(seed, part) draws one part's arguments, and reference() takes and returns one part's arrays. A program takes and returns all parts, laid end to end along the dimension named above; an argument that names none is the same for every part. Nothing has to cross between parts.
All inputs are finite; a program needn't handle non-finite values.
Results may differ from the reference program's by a relative error of at most 0.01575.
Values may be sent and summed in bfloat16 or wider, within the bound.
A program may use at most 64 MiB of HBM per device.

```python
import math
import jax
import jax.numpy as jnp
from jax import lax

D = 1024
H = 16
HD = 64
LAT = 2048
SEQ = 4096


def draw_queries(key, part):
    base = jnp.clip(jax.random.normal(key, (H, HD, LAT), jnp.float32), -6.0, 6.0)
    return base.astype(jnp.bfloat16)


def block_levels(stream_key, extent, cuts, low, high):
    level = 1.0
    for position, shards_of in cuts:
        steps = jax.random.uniform(jax.random.fold_in(jax.random.fold_in(stream_key, 6), position), (shards_of,), jnp.float32, low / len(cuts), high / len(cuts))
        level = level * jnp.repeat(jnp.exp(steps), extent[position] // shards_of).reshape((-1,) + (1,) * (len(extent) - 1 - position))
    return level


def normal_values(rng, extent, deviation, bound, split=(), kind=jnp.bfloat16):
    level = block_levels(rng, extent, split, -0.22, 0.18) if split else 1.0
    result = jax.random.normal(rng, extent, jnp.float32) * deviation * level
    return jnp.minimum(jnp.maximum(result, -bound), bound).astype(kind)


def setup_inputs(seed: int = 0, part: int = 0) -> dict:
    key_of = jax.random.split(jax.random.key(seed), 6)
    part_keys = jax.random.split(jax.random.fold_in(key_of[5], part), 6)
    context = normal_values(part_keys[0], (SEQ, D), 1.0, 6.0, ((0, 16),))
    w_kv = normal_values(key_of[1], (D, 2 * D), D ** -0.5, 0.1875)
    queries = draw_queries(jax.random.fold_in(jax.random.fold_in(key_of[5], part), 71), part)
    gain = jnp.clip(1.0 + 0.15 * jax.random.normal(key_of[3], (D,), jnp.float32), 0.25, 1.75)
    w_out = normal_values(key_of[4], (D, D), D ** -0.5, 0.1875, ((0, 4),))
    return {"context": context, "w_kv": w_kv, "queries": queries, "gain": gain, "w_out": w_out}


def head_attention(query_head, kv_head):
    block_size = 256
    block_count = LAT // block_size
    key_rows = kv_head[:, :HD]
    value_rows = kv_head[:, HD:]
    head_scale = 1.0 / math.sqrt(HD)
    query_blocks = query_head.reshape(HD, block_count, block_size).transpose(1, 0, 2)

    def one_block(query_block):
        scores = jnp.dot(query_block.T, key_rows.T, preferred_element_type=jnp.float32) * head_scale
        highest = lax.optimization_barrier(jnp.max(scores, axis=1, keepdims=True))
        weights = jnp.exp(scores - highest)
        row_total = lax.optimization_barrier(jnp.sum(weights, axis=1, keepdims=True))
        summed = jnp.dot(weights.astype(jnp.bfloat16), value_rows, preferred_element_type=jnp.float32)
        return summed / row_total
    outputs = lax.map(one_block, query_blocks)
    return outputs.reshape(LAT, HD)

def reference(context, w_kv, queries, gain, w_out):
    projected = jnp.dot(context, w_kv, preferred_element_type=jnp.float32).astype(jnp.bfloat16)
    kv_heads = projected.reshape(SEQ, H, 2 * HD).transpose(1, 0, 2)
    heads_out = lax.map(lambda pair: head_attention(pair[0], pair[1]), (queries, kv_heads))
    attended = heads_out.transpose(1, 0, 2).reshape(LAT, D)
    mean_square = lax.optimization_barrier(jnp.mean(attended * attended, axis=1, keepdims=True))
    normed = (attended * gain[None, :] * lax.rsqrt(mean_square + 1e-06)).astype(jnp.bfloat16)
    return jnp.dot(normed, w_out, preferred_element_type=jnp.float32).astype(jnp.bfloat16)
```

```python
import functools
import math

import jax
import jax.numpy as jnp
from jax import lax
from jax.experimental import pallas as pl
from jax.experimental.pallas import tpu as pltpu
from jax.sharding import PartitionSpec as P

epsilon = 1e-06
MESH = pl.DeviceIdType.MESH


def attention_kernel(
    n_head, n_ctx, q_tile,
    context_ref, w_kv_ref, queries_ref, gain_ref,
    normed_ref,
    kv_send, kv_all, acc, high, total, head_out, head_in, *rest,
):
    n_stage = n_ctx.bit_length() - 1
    sum_send, rest = rest[:n_stage], rest[n_stage:]
    sum_recv, rest = rest[:n_stage], rest[n_stage:]
    stat_send, rest = rest[:n_stage], rest[n_stage:]
    stat_recv, rest = rest[:n_stage], rest[n_stage:]
    kv_ssem, kv_rsem, sum_ssem, sum_rsem, stat_ssem, stat_rsem, out_ssem, out_rsem = rest

    heads_local, head_size, latents = queries_ref.shape
    width = 2 * head_size
    group_width = heads_local * width
    ctx_rows = latents // n_ctx
    own_rows = ctx_rows // n_head
    scale = math.log2(math.e) / math.sqrt(head_size)
    my_head = lax.axis_index("head")
    my_ctx = lax.axis_index("ctx")

    barrier = pltpu.get_barrier_semaphore()
    for mask in range(1, n_head):
        pl.semaphore_signal(
            barrier, inc=1, device_id={"head": my_head ^ mask}, device_id_type=MESH
        )
    for stage in range(n_stage):
        pl.semaphore_signal(
            barrier, inc=1, device_id={"ctx": my_ctx ^ (1 << stage)}, device_id_type=MESH
        )

    def project(target):
        columns = pl.ds(pl.multiple_of(target * group_width, group_width), group_width)
        return jnp.dot(
            context_ref[...], w_kv_ref[:, columns], preferred_element_type=jnp.float32
        ).astype(jnp.bfloat16)

    kv_copies = {}
    for mask in range(n_head - 1, 0, -1):
        kv_send[mask - 1] = project(my_head ^ mask)
        if mask == n_head - 1:
            pl.semaphore_wait(barrier, n_head - 1 + n_stage)
        kv_copies[mask] = pltpu.make_async_remote_copy(
            src_ref=kv_send.at[mask - 1],
            dst_ref=kv_all.at[mask],
            send_sem=kv_ssem.at[mask - 1],
            recv_sem=kv_rsem.at[mask - 1],
            device_id={"head": my_head ^ mask},
            device_id_type=MESH,
        )
        kv_copies[mask].start()
    kv_all[0] = project(my_head)

    def attend(slot, head, first):
        columns = pl.ds(pl.multiple_of(head * width, width), width)
        block = kv_all[slot, :, columns]
        key = block[:, :head_size]
        value = block.T[head_size:, :]
        for tile in range(latents // q_tile):
            span = slice(tile * q_tile, (tile + 1) * q_tile)
            scores = (
                jnp.dot(key, queries_ref[head, :, span], preferred_element_type=jnp.float32)
                * scale
            )
            highest = jnp.max(scores, axis=0, keepdims=True)
            if not first:
                before = high[head, :, span]
                highest = jnp.maximum(highest, before)
                factor = jnp.exp2(before - highest)
            weights = jnp.exp2(scores - highest)
            row_total = jnp.sum(weights, axis=0, keepdims=True)
            summed = jnp.dot(
                value, weights.astype(jnp.bfloat16), preferred_element_type=jnp.float32
            )
            if not first:
                row_total += total[head, :, span] * factor
                summed += acc[head, :, span] * factor
            high[head, :, span] = highest
            total[head, :, span] = row_total
            acc[head, :, span] = summed

    order = [0] + ([1] if n_head > 1 else []) + list(range(n_head - 1, 1, -1))
    for slot in order[:-1]:
        if slot:
            kv_copies[slot].wait_recv()

        def one_head(head, carry, slot=slot):
            attend(slot, head, slot == 0)
            return carry

        lax.fori_loop(0, heads_local, one_head, 0)
    last = order[-1]
    if last:
        kv_copies[last].wait_recv()

    copies = []
    pending = {}
    held = {}

    def chunk(head, stage, index):
        if stage == 0:
            span = pl.ds(pl.multiple_of(index * ctx_rows, ctx_rows), ctx_rows)
            return acc[head, :, span], high[head, :, span], total[head, :, span]
        source = pl.ds(pl.multiple_of(index * ctx_rows, ctx_rows), ctx_rows)
        return acc[head, :, source], high[head, :, source], total[head, :, source]

    def send_stage(head, stage):
        bit = (my_ctx >> stage) & 1
        for t in range(n_ctx >> (stage + 1)):
            value, top, weight = chunk(head, stage, 2 * t + 1 - bit)
            span = slice(t * ctx_rows, (t + 1) * ctx_rows)
            sum_send[stage][head, :, span] = value.astype(jnp.bfloat16)
            stat_send[stage][head, 0:1, span] = top
            stat_send[stage][head, 1:2, span] = weight
        pair = []
        for source, target, ssem, rsem in (
            (sum_send, sum_recv, sum_ssem, sum_rsem),
            (stat_send, stat_recv, stat_ssem, stat_rsem),
        ):
            copy = pltpu.make_async_remote_copy(
                src_ref=source[stage].at[head],
                dst_ref=target[stage].at[head],
                send_sem=ssem.at[stage, head],
                recv_sem=rsem.at[stage, head],
                device_id={"ctx": my_ctx ^ (1 << stage)},
                device_id_type=MESH,
            )
            copy.start()
            pair.append(copy)
        copies.extend(pair)
        pending[head, stage] = pair

    def merge_stage(head, stage):
        for copy in pending[head, stage]:
            copy.wait_recv()
        bit = (my_ctx >> stage) & 1
        merged = []
        for t in range(n_ctx >> (stage + 1)):
            value, top, weight = chunk(head, stage, 2 * t + bit)
            span = slice(t * ctx_rows, (t + 1) * ctx_rows)
            other = sum_recv[stage][head, :, span].astype(jnp.float32)
            other_top = stat_recv[stage][head, 0:1, span]
            other_weight = stat_recv[stage][head, 1:2, span]
            highest = jnp.maximum(top, other_top)
            mine = jnp.exp2(top - highest)
            theirs = jnp.exp2(other_top - highest)
            merged.append((
                value * mine + other * theirs,
                highest,
                weight * mine + other_weight * theirs,
            ))
            if stage + 1 < n_stage:
                acc[head, :, span], high[head, :, span], total[head, :, span] = merged[-1]
        return merged[0]

    def send_out(head, value, weight):
        attended = (value / weight).astype(jnp.bfloat16)
        for piece in range(n_head):
            head_out[piece, head] = attended[:, piece * own_rows:(piece + 1) * own_rows]
        for mask in range(1, n_head):
            copy = pltpu.make_async_remote_copy(
                src_ref=head_out.at[my_head ^ mask, head],
                dst_ref=head_in.at[my_head, head],
                send_sem=out_ssem.at[mask - 1, head],
                recv_sem=out_rsem.at[mask - 1, head],
                device_id={"head": my_head ^ mask},
                device_id_type=MESH,
            )
            copy.start()
            copies.append(copy)
            pending["out", head, mask] = copy
        head_in[my_head, head] = head_out[my_head, head]

    def advance(head, stage):
        merged = merge_stage(head, stage)
        if stage + 1 < n_stage:
            send_stage(head, stage + 1)
        else:
            send_out(head, merged[0], merged[2])

    for step in range(heads_local + n_stage):
        if step < heads_local:
            attend(last, step, last == 0)
            send_stage(step, 0)
        for stage in range(n_stage):
            head = step - 1 - stage
            if 0 <= head < heads_local:
                advance(head, stage)

    for head in range(heads_local):
        for mask in range(1, n_head):
            pending["out", head, mask].wait_recv()
    joined = head_in[...].astype(jnp.float32).reshape(
        n_head * heads_local * head_size, own_rows
    )
    mean_square = jnp.sum(joined * joined, axis=0, keepdims=True) / joined.shape[0]
    normed_ref[...] = (
        joined * gain_ref[...] * lax.rsqrt(mean_square + epsilon)
    ).astype(jnp.bfloat16)

    for mask in range(1, n_head):
        kv_copies[mask].wait_send()
    for copy in copies:
        copy.wait_send()


def body(context, w_kv, queries, gain, w_out):
    heads_local, head_size, latents = queries.shape
    model_width = w_kv.shape[0]
    n_head = lax.axis_size("head")
    n_ctx = lax.axis_size("ctx")
    n_stage = n_ctx.bit_length() - 1
    rows = context.shape[0]
    ctx_rows = latents // n_ctx
    own_rows = ctx_rows // n_head
    group_width = heads_local * 2 * head_size
    w_full = lax.all_gather(w_out, "head", axis=0, tiled=True)

    def stage_buffers(depth, kind):
        return [
            pltpu.VMEM((heads_local, depth, (n_ctx >> (s + 1)) * ctx_rows), kind)
            for s in range(n_stage)
        ]

    dma = pltpu.SemaphoreType.DMA
    vmem = pl.BlockSpec(memory_space=pltpu.VMEM)
    normed = pl.pallas_call(
        functools.partial(attention_kernel, n_head, n_ctx, min(512, latents)),
        out_shape=jax.ShapeDtypeStruct((model_width, own_rows), jnp.bfloat16),
        in_specs=[vmem] * 4,
        out_specs=vmem,
        scratch_shapes=[
            pltpu.VMEM((n_head - 1, rows, group_width), jnp.bfloat16),
            pltpu.VMEM((n_head, rows, group_width), jnp.bfloat16),
            pltpu.VMEM((heads_local, head_size, latents), jnp.float32),
            pltpu.VMEM((heads_local, 1, latents), jnp.float32),
            pltpu.VMEM((heads_local, 1, latents), jnp.float32),
            pltpu.VMEM((n_head, heads_local, head_size, own_rows), jnp.bfloat16),
            pltpu.VMEM((n_head, heads_local, head_size, own_rows), jnp.bfloat16),
            *stage_buffers(head_size, jnp.bfloat16),
            *stage_buffers(head_size, jnp.bfloat16),
            *stage_buffers(2, jnp.float32),
            *stage_buffers(2, jnp.float32),
            dma((n_head - 1,)),
            dma((n_head - 1,)),
            dma((n_stage, heads_local)),
            dma((n_stage, heads_local)),
            dma((n_stage, heads_local)),
            dma((n_stage, heads_local)),
            dma((n_head - 1, heads_local)),
            dma((n_head - 1, heads_local)),
        ],
        compiler_params=pltpu.CompilerParams(
            collective_id=0, has_side_effects=True, vmem_limit_bytes=48 * 1024 * 1024
        ),
        cost_estimate=pl.CostEstimate(
            flops=4 * heads_local * latents * rows * n_head * head_size
            + 4 * rows * model_width * model_width,
            bytes_accessed=2 * w_kv.size + 2 * context.size + 2 * queries.size,
            transcendentals=heads_local * latents * rows * n_head,
        ),
    )(context, w_kv, queries, gain.reshape(model_width, 1))
    result = lax.dot_general(
        normed, w_full, (((0,), (0,)), ((), ())), preferred_element_type=jnp.float32
    )
    return result.astype(jnp.bfloat16)


def solution(mesh):
    return jax.shard_map(
        body,
        mesh=mesh,
        in_specs=(
            P(("groups", "ctx", "head"), None),
            P(),
            P(("groups", "head"), None, None),
            P(),
            P("head", None),
        ),
        out_specs=P(("groups", "ctx", "head"), None),
        check_vma=False,
    )
```

```python
import functools
import math

import jax
import jax.numpy as jnp
from jax import lax
from jax.experimental import pallas as pl
from jax.experimental.pallas import tpu as pltpu
from jax.sharding import PartitionSpec as P

epsilon = 1e-06
MESH = pl.DeviceIdType.MESH


def attention_kernel(
    n_head, n_ctx, n_part, q_tile,
    context_ref, w_kv_ref, queries_ref, gain_ref, w_out_ref,
    out_ref,
    kv_send, kv_all, acc, high, total, head_out, head_in, w_all, *rest,
):
    n_stage = n_ctx.bit_length() - 1
    sum_send, rest = rest[:n_stage], rest[n_stage:]
    sum_recv, rest = rest[:n_stage], rest[n_stage:]
    stat_send, rest = rest[:n_stage], rest[n_stage:]
    stat_recv, rest = rest[:n_stage], rest[n_stage:]
    kv_ssem, kv_rsem, sum_ssem, sum_rsem, stat_ssem, stat_rsem, out_ssem, out_rsem = rest[:8]
    wh_ssem, wh_rsem, wp_ssem, wp_rsem = rest[8:]

    heads_local, head_size, latents = queries_ref.shape
    width = 2 * head_size
    group_width = heads_local * width
    ctx_rows = latents // n_ctx
    own_rows = ctx_rows // n_head
    scale = math.log2(math.e) / math.sqrt(head_size)
    my_head = lax.axis_index("head")
    my_ctx = lax.axis_index("ctx")
    my_group = lax.axis_index("groups")
    ctx_parts = min(n_ctx, n_part)
    group_bits = (n_part // ctx_parts).bit_length() - 1
    my_part = (my_group & ((1 << group_bits) - 1)) * ctx_parts + (my_ctx & (ctx_parts - 1))
    part_width = w_all.shape[3]

    barrier = pltpu.get_barrier_semaphore()
    for mask in range(1, n_head):
        pl.semaphore_signal(
            barrier, inc=1, device_id={"head": my_head ^ mask}, device_id_type=MESH
        )
    for stage in range(n_stage):
        pl.semaphore_signal(
            barrier, inc=1, device_id={"ctx": my_ctx ^ (1 << stage)}, device_id_type=MESH
        )
    for level in range(group_bits):
        pl.semaphore_signal(
            barrier, inc=1, device_id={"groups": my_group ^ (1 << level)}, device_id_type=MESH
        )
    part_span = pl.ds(pl.multiple_of(my_part * part_width, part_width), part_width)
    w_all[0, my_head] = w_out_ref[:, part_span]

    def project(target):
        columns = pl.ds(pl.multiple_of(target * group_width, group_width), group_width)
        return jnp.dot(
            context_ref[...], w_kv_ref[:, columns], preferred_element_type=jnp.float32
        ).astype(jnp.bfloat16)

    weight_copies = []
    w_pending = {}

    def send_w(key, source, target, ssem, rsem, where):
        copy = pltpu.make_async_remote_copy(
            src_ref=source,
            dst_ref=target,
            send_sem=ssem,
            recv_sem=rsem,
            device_id=where,
            device_id_type=MESH,
        )
        copy.start()
        weight_copies.append(copy)
        w_pending.setdefault(key, []).append(copy)

    def receive_w(key):
        for copy in w_pending[key]:
            copy.wait_recv()

    head_levels = list(reversed(range(n_head.bit_length() - 1)))
    part_levels = list(reversed(range(n_part.bit_length() - 1)))
    w_masks = {"head": [0], "part": [0]}

    def w_head(level):
        bit = 1 << level
        for mask in w_masks["head"]:
            index = (mask | bit) - 1
            block = w_all.at[0, my_head ^ mask]
            send_w(
                ("head", level), block, block,
                wh_ssem.at[index], wh_rsem.at[index], {"head": my_head ^ bit},
            )
        w_masks["head"] += [mask | bit for mask in w_masks["head"]]

    def w_part(level):
        bit = 1 << level
        if bit >= ctx_parts:
            where = {"groups": my_group ^ (bit // ctx_parts)}
        else:
            where = {"ctx": my_ctx ^ bit}
        for mask in w_masks["part"]:
            index = (mask | bit) - 1
            send_w(
                ("part", level), w_all.at[mask], w_all.at[mask | bit],
                wp_ssem.at[index], wp_rsem.at[index], where,
            )
        w_masks["part"] += [mask | bit for mask in w_masks["part"]]

    w_steps = [("head", level) for level in head_levels]
    w_steps += [("part", level) for level in part_levels]
    w_done = [0]

    def advance_w():
        index = w_done[0]
        if index > len(w_steps):
            return
        if index:
            receive_w(w_steps[index - 1])
        if index < len(w_steps):
            kind, level = w_steps[index]
            (w_head if kind == "head" else w_part)(level)
        w_done[0] = index + 1

    near = [1] if n_head > 1 else []
    far = list(range(n_head - 1, 1, -1))
    kv_copies = {}

    def send_kv(mask, head):
        kv_copies[mask, head] = pltpu.make_async_remote_copy(
            src_ref=kv_send.at[mask - 1, head],
            dst_ref=kv_all.at[mask, head],
            send_sem=kv_ssem.at[mask - 1, head],
            recv_sem=kv_rsem.at[mask - 1, head],
            device_id={"head": my_head ^ mask},
            device_id_type=MESH,
        )
        kv_copies[mask, head].start()

    def project_into(mask, target):
        projected = project(my_head ^ mask)
        for head in range(heads_local):
            target[mask - 1 if mask else 0, head] = projected[:, head * width:(head + 1) * width]

    for mask in far + near:
        project_into(mask, kv_send)
        if mask == (far + near)[0]:
            pl.semaphore_wait(barrier, n_head - 1 + n_stage + group_bits)
            advance_w()
        if len(far) > 1 and mask == far[0]:
            send_kv(mask, 0)
        elif far and mask == far[-1]:
            for head in range(heads_local):
                for other in far:
                    if (other, head) not in kv_copies:
                        send_kv(other, head)
        elif mask == 1:
            for head in range(heads_local):
                send_kv(1, head)
    project_into(0, kv_all)

    def attend(slot, head, first):
        block = kv_all[slot, head]
        key = block[:, :head_size]
        value = block.T[head_size:, :]
        for tile in range(latents // q_tile):
            span = slice(tile * q_tile, (tile + 1) * q_tile)
            scores = (
                jnp.dot(key, queries_ref[head, :, span], preferred_element_type=jnp.float32)
                * scale
            )
            highest = jnp.max(scores, axis=0, keepdims=True)
            if not first:
                before = high[head, :, span]
                highest = jnp.maximum(highest, before)
                factor = jnp.exp2(before - highest)
            weights = jnp.exp2(scores - highest)
            row_total = jnp.sum(weights, axis=0, keepdims=True)
            summed = jnp.dot(
                value, weights.astype(jnp.bfloat16), preferred_element_type=jnp.float32
            )
            if not first:
                row_total += total[head, :, span] * factor
                summed += acc[head, :, span] * factor
            high[head, :, span] = highest
            total[head, :, span] = row_total
            acc[head, :, span] = summed

    for slot in [0] + near:
        if slot:
            advance_w()
            for head in range(heads_local):
                kv_copies[slot, head].wait_recv()

        def one_head(head, carry, slot=slot):
            attend(slot, head, slot == 0)
            return carry

        lax.fori_loop(0, heads_local, one_head, 0)

    copies = []
    pending = {}
    held = {}

    def chunk(head, stage, index):
        if stage == 0:
            span = pl.ds(pl.multiple_of(index * ctx_rows, ctx_rows), ctx_rows)
            return acc[head, :, span], high[head, :, span], total[head, :, span]
        source = pl.ds(pl.multiple_of(index * ctx_rows, ctx_rows), ctx_rows)
        return acc[head, :, source], high[head, :, source], total[head, :, source]

    def send_stage(head, stage):
        bit = (my_ctx >> stage) & 1
        for t in range(n_ctx >> (stage + 1)):
            value, top, weight = chunk(head, stage, 2 * t + 1 - bit)
            span = slice(t * ctx_rows, (t + 1) * ctx_rows)
            sum_send[stage][head, :, span] = value.astype(jnp.bfloat16)
            stat_send[stage][head, 0:1, span] = top
            stat_send[stage][head, 1:2, span] = weight
        pair = []
        for source, target, ssem, rsem in (
            (sum_send, sum_recv, sum_ssem, sum_rsem),
            (stat_send, stat_recv, stat_ssem, stat_rsem),
        ):
            copy = pltpu.make_async_remote_copy(
                src_ref=source[stage].at[head],
                dst_ref=target[stage].at[head],
                send_sem=ssem.at[stage, head],
                recv_sem=rsem.at[stage, head],
                device_id={"ctx": my_ctx ^ (1 << stage)},
                device_id_type=MESH,
            )
            copy.start()
            pair.append(copy)
        copies.extend(pair)
        pending[head, stage] = pair

    def merge_stage(head, stage):
        for copy in pending[head, stage]:
            copy.wait_recv()
        bit = (my_ctx >> stage) & 1
        merged = []
        for t in range(n_ctx >> (stage + 1)):
            value, top, weight = chunk(head, stage, 2 * t + bit)
            span = slice(t * ctx_rows, (t + 1) * ctx_rows)
            other = sum_recv[stage][head, :, span].astype(jnp.float32)
            other_top = stat_recv[stage][head, 0:1, span]
            other_weight = stat_recv[stage][head, 1:2, span]
            highest = jnp.maximum(top, other_top)
            mine = jnp.exp2(top - highest)
            theirs = jnp.exp2(other_top - highest)
            merged.append((
                value * mine + other * theirs,
                highest,
                weight * mine + other_weight * theirs,
            ))
            if stage + 1 < n_stage:
                acc[head, :, span], high[head, :, span], total[head, :, span] = merged[-1]
        return merged[0]

    def send_out(head, value, weight):
        attended = (value / weight).astype(jnp.bfloat16)
        for piece in range(n_head):
            head_out[piece, head] = attended[:, piece * own_rows:(piece + 1) * own_rows]
        for mask in range(1, n_head):
            copy = pltpu.make_async_remote_copy(
                src_ref=head_out.at[my_head ^ mask, head],
                dst_ref=head_in.at[my_head, head],
                send_sem=out_ssem.at[mask - 1, head],
                recv_sem=out_rsem.at[mask - 1, head],
                device_id={"head": my_head ^ mask},
                device_id_type=MESH,
            )
            copy.start()
            copies.append(copy)
            pending["out", head, mask] = copy
        head_in[my_head, head] = head_out[my_head, head]

    def advance(head, stage):
        merged = merge_stage(head, stage)
        if stage + 1 < n_stage:
            send_stage(head, stage + 1)
        else:
            send_out(head, merged[0], merged[2])

    for step in range(heads_local + n_stage):
        if step < heads_local:
            advance_w()
            for mask in far:
                kv_copies[mask, step].wait_recv()
                attend(mask, step, False)
            send_stage(step, 0)
        for stage in range(n_stage):
            head = step - 1 - stage
            if 0 <= head < heads_local:
                advance(head, stage)

    while w_done[0] <= len(w_steps):
        advance_w()
    for head in range(heads_local):
        for mask in range(1, n_head):
            pending["out", head, mask].wait_recv()
    joined = head_in[...].astype(jnp.float32).reshape(
        n_head * heads_local * head_size, own_rows
    )
    mean_square = jnp.sum(joined * joined, axis=0, keepdims=True) / joined.shape[0]
    normed = (joined * gain_ref[...] * lax.rsqrt(mean_square + epsilon)).astype(jnp.bfloat16)
    rows = normed.T
    for mask in range(n_part):
        weights = w_all[mask].reshape(joined.shape[0], part_width)
        target = pl.ds(pl.multiple_of((my_part ^ mask) * part_width, part_width), part_width)
        out_ref[:, target] = jnp.dot(
            rows, weights, preferred_element_type=jnp.float32
        ).astype(jnp.bfloat16)

    for copy in list(kv_copies.values()) + weight_copies + copies:
        copy.wait_send()


def body(context, w_kv, queries, gain, w_out):
    heads_local, head_size, latents = queries.shape
    model_width = w_kv.shape[0]
    n_head = lax.axis_size("head")
    n_ctx = lax.axis_size("ctx")
    n_stage = n_ctx.bit_length() - 1
    rows = context.shape[0]
    ctx_rows = latents // n_ctx
    own_rows = ctx_rows // n_head
    n_part = min(lax.axis_size("groups") * n_ctx, model_width // 128)

    def stage_buffers(depth, kind):
        return [
            pltpu.VMEM((heads_local, depth, (n_ctx >> (s + 1)) * ctx_rows), kind)
            for s in range(n_stage)
        ]

    dma = pltpu.SemaphoreType.DMA
    vmem = pl.BlockSpec(memory_space=pltpu.VMEM)
    return pl.pallas_call(
        functools.partial(attention_kernel, n_head, n_ctx, n_part, min(1024, latents)),
        out_shape=jax.ShapeDtypeStruct((own_rows, model_width), jnp.bfloat16),
        in_specs=[vmem] * 5,
        out_specs=vmem,
        scratch_shapes=[
            pltpu.VMEM((n_head - 1, heads_local, rows, 2 * head_size), jnp.bfloat16),
            pltpu.VMEM((n_head, heads_local, rows, 2 * head_size), jnp.bfloat16),
            pltpu.VMEM((heads_local, head_size, latents), jnp.float32),
            pltpu.VMEM((heads_local, 1, latents), jnp.float32),
            pltpu.VMEM((heads_local, 1, latents), jnp.float32),
            pltpu.VMEM((n_head, heads_local, head_size, own_rows), jnp.bfloat16),
            pltpu.VMEM((n_head, heads_local, head_size, own_rows), jnp.bfloat16),
            pltpu.VMEM(
                (n_part, n_head, w_out.shape[0], model_width // n_part), jnp.bfloat16
            ),
            *stage_buffers(head_size, jnp.bfloat16),
            *stage_buffers(head_size, jnp.bfloat16),
            *stage_buffers(2, jnp.float32),
            *stage_buffers(2, jnp.float32),
            dma((n_head - 1, heads_local)),
            dma((n_head - 1, heads_local)),
            dma((n_stage, heads_local)),
            dma((n_stage, heads_local)),
            dma((n_stage, heads_local)),
            dma((n_stage, heads_local)),
            dma((n_head - 1, heads_local)),
            dma((n_head - 1, heads_local)),
            dma((n_head - 1,)),
            dma((n_head - 1,)),
            dma((n_part - 1,)),
            dma((n_part - 1,)),
        ],
        compiler_params=pltpu.CompilerParams(
            collective_id=0, has_side_effects=True, vmem_limit_bytes=48 * 1024 * 1024
        ),
        cost_estimate=pl.CostEstimate(
            flops=4 * heads_local * latents * rows * n_head * head_size
            + 4 * rows * model_width * model_width,
            bytes_accessed=2 * w_kv.size + 2 * context.size + 2 * queries.size,
            transcendentals=heads_local * latents * rows * n_head,
        ),
    )(context, w_kv, queries, gain.reshape(model_width, 1), w_out)


def solution(mesh):
    return jax.shard_map(
        body,
        mesh=mesh,
        in_specs=(
            P(("groups", "ctx", "head"), None),
            P(),
            P(("groups", "head"), None, None),
            P(),
            P("head", None),
        ),
        out_specs=P(("groups", "ctx", "head"), None),
        check_vma=False,
    )
```

```python
import functools
import math

import jax
import jax.numpy as jnp
from jax import lax
from jax.experimental import pallas as pl
from jax.experimental.pallas import tpu as pltpu
from jax.sharding import PartitionSpec as P

epsilon = 1e-06
MESH = pl.DeviceIdType.MESH


def attention_kernel(
    n_head, n_ctx, n_part, q_tile,
    context_ref, w_kv_ref, queries_ref, gain_ref, w_out_ref,
    out_ref,
    kv_send, kv_all, acc, high, total, head_out, head_in, w_all, *rest,
):
    n_stage = n_ctx.bit_length() - 1
    sum_send, rest = rest[:n_stage], rest[n_stage:]
    sum_recv, rest = rest[:n_stage], rest[n_stage:]
    stat_send, rest = rest[:n_stage], rest[n_stage:]
    stat_recv, rest = rest[:n_stage], rest[n_stage:]
    kv_ssem, kv_rsem, sum_ssem, sum_rsem, stat_ssem, stat_rsem, out_ssem, out_rsem = rest[:8]
    wh_ssem, wh_rsem, wp_ssem, wp_rsem = rest[8:]

    heads_local, head_size, latents = queries_ref.shape
    width = 2 * head_size
    group_width = heads_local * width
    ctx_rows = latents // n_ctx
    own_rows = ctx_rows // n_head
    scale = math.log2(math.e) / math.sqrt(head_size)
    my_head = lax.axis_index("head")
    my_ctx = lax.axis_index("ctx")
    my_group = lax.axis_index("groups")
    ctx_parts = min(n_ctx, n_part)
    group_bits = (n_part // ctx_parts).bit_length() - 1
    my_part = (my_group & ((1 << group_bits) - 1)) * ctx_parts + (my_ctx & (ctx_parts - 1))
    part_width = w_all.shape[3]

    barrier = pltpu.get_barrier_semaphore()
    for mask in range(1, n_head):
        pl.semaphore_signal(
            barrier, inc=1, device_id={"head": my_head ^ mask}, device_id_type=MESH
        )
    for stage in range(n_stage):
        pl.semaphore_signal(
            barrier, inc=1, device_id={"ctx": my_ctx ^ (1 << stage)}, device_id_type=MESH
        )
    for level in range(group_bits):
        pl.semaphore_signal(
            barrier, inc=1, device_id={"groups": my_group ^ (1 << level)}, device_id_type=MESH
        )
    part_span = pl.ds(pl.multiple_of(my_part * part_width, part_width), part_width)
    w_all[0, my_head] = w_out_ref[:, part_span]

    def project(target):
        columns = pl.ds(pl.multiple_of(target * group_width, group_width), group_width)
        return jnp.dot(
            context_ref[...], w_kv_ref[:, columns], preferred_element_type=jnp.float32
        ).astype(jnp.bfloat16)

    weight_copies = []
    w_pending = {}

    def send_w(key, source, target, ssem, rsem, where):
        copy = pltpu.make_async_remote_copy(
            src_ref=source,
            dst_ref=target,
            send_sem=ssem,
            recv_sem=rsem,
            device_id=where,
            device_id_type=MESH,
        )
        copy.start()
        weight_copies.append(copy)
        w_pending.setdefault(key, []).append(copy)

    def receive_w(key):
        for copy in w_pending[key]:
            copy.wait_recv()

    part_levels = list(reversed(range(n_part.bit_length() - 1)))
    part_masks = [0]

    def w_head(level):
        for mask in range(n_head - 1, 0, -1):
            block = w_all.at[0, my_head]
            send_w(
                ("head", level), block, block,
                wh_ssem.at[mask - 1], wh_rsem.at[mask - 1], {"head": my_head ^ mask},
            )

    def w_part(level):
        bit = 1 << level
        if bit >= ctx_parts:
            where = {"groups": my_group ^ (bit // ctx_parts)}
        else:
            where = {"ctx": my_ctx ^ bit}
        for mask in part_masks:
            index = (mask | bit) - 1
            send_w(
                ("part", level), w_all.at[mask], w_all.at[mask | bit],
                wp_ssem.at[index], wp_rsem.at[index], where,
            )
        part_masks.extend([mask | bit for mask in part_masks])

    w_steps = [("head", 0)]
    w_steps += [("part", level) for level in part_levels]
    w_done = [0]

    def advance_w():
        index = w_done[0]
        if index > len(w_steps):
            return
        if index:
            receive_w(w_steps[index - 1])
        if index < len(w_steps):
            kind, level = w_steps[index]
            (w_head if kind == "head" else w_part)(level)
        w_done[0] = index + 1

    near = [1] if n_head > 1 else []
    far = list(range(n_head - 1, 1, -1))
    kv_copies = {}

    def send_kv(mask, head):
        kv_copies[mask, head] = pltpu.make_async_remote_copy(
            src_ref=kv_send.at[mask - 1, head],
            dst_ref=kv_all.at[mask, head],
            send_sem=kv_ssem.at[mask - 1, head],
            recv_sem=kv_rsem.at[mask - 1, head],
            device_id={"head": my_head ^ mask},
            device_id_type=MESH,
        )
        kv_copies[mask, head].start()

    def project_into(mask, target):
        projected = project(my_head ^ mask)
        for head in range(heads_local):
            target[mask - 1 if mask else 0, head] = projected[:, head * width:(head + 1) * width]

    for mask in far + near:
        project_into(mask, kv_send)
        if mask == (far + near)[0]:
            pl.semaphore_wait(barrier, n_head - 1 + n_stage + group_bits)
            advance_w()
        if len(far) > 1 and mask == far[0]:
            send_kv(mask, 0)
        elif far and mask == far[-1]:
            for head in range(heads_local):
                for other in far:
                    if (other, head) not in kv_copies:
                        send_kv(other, head)
        elif mask == 1:
            for head in range(heads_local):
                send_kv(1, head)
    project_into(0, kv_all)

    def attend(slot, head, first):
        block = kv_all[slot, head]
        key = block[:, :head_size]
        value = block.T[head_size:, :]
        for tile in range(latents // q_tile):
            span = slice(tile * q_tile, (tile + 1) * q_tile)
            scores = (
                jnp.dot(key, queries_ref[head, :, span], preferred_element_type=jnp.float32)
                * scale
            )
            highest = jnp.max(scores, axis=0, keepdims=True)
            if not first:
                before = high[head, :, span]
                highest = jnp.maximum(highest, before)
                factor = jnp.exp2(before - highest)
            weights = jnp.exp2(scores - highest)
            row_total = jnp.sum(weights, axis=0, keepdims=True)
            summed = jnp.dot(
                value, weights.astype(jnp.bfloat16), preferred_element_type=jnp.float32
            )
            if not first:
                row_total += total[head, :, span] * factor
                summed += acc[head, :, span] * factor
            high[head, :, span] = highest
            total[head, :, span] = row_total
            acc[head, :, span] = summed

    for slot in [0] + near:
        if slot:
            advance_w()
            for head in range(heads_local):
                kv_copies[slot, head].wait_recv()

        def one_head(head, carry, slot=slot):
            attend(slot, head, slot == 0)
            return carry

        lax.fori_loop(0, heads_local, one_head, 0)

    copies = []
    pending = {}
    held = {}

    def chunk(head, stage, index):
        if stage == 0:
            span = pl.ds(pl.multiple_of(index * ctx_rows, ctx_rows), ctx_rows)
            return acc[head, :, span], high[head, :, span], total[head, :, span]
        source = pl.ds(pl.multiple_of(index * ctx_rows, ctx_rows), ctx_rows)
        return acc[head, :, source], high[head, :, source], total[head, :, source]

    def send_stage(head, stage):
        bit = (my_ctx >> stage) & 1
        for t in range(n_ctx >> (stage + 1)):
            value, top, weight = chunk(head, stage, 2 * t + 1 - bit)
            span = slice(t * ctx_rows, (t + 1) * ctx_rows)
            sum_send[stage][head, :, span] = value.astype(jnp.bfloat16)
            stat_send[stage][head, 0:1, span] = top
            stat_send[stage][head, 1:2, span] = weight
        pair = []
        for source, target, ssem, rsem in (
            (sum_send, sum_recv, sum_ssem, sum_rsem),
            (stat_send, stat_recv, stat_ssem, stat_rsem),
        ):
            copy = pltpu.make_async_remote_copy(
                src_ref=source[stage].at[head],
                dst_ref=target[stage].at[head],
                send_sem=ssem.at[stage, head],
                recv_sem=rsem.at[stage, head],
                device_id={"ctx": my_ctx ^ (1 << stage)},
                device_id_type=MESH,
            )
            copy.start()
            pair.append(copy)
        copies.extend(pair)
        pending[head, stage] = pair

    def merge_stage(head, stage):
        for copy in pending[head, stage]:
            copy.wait_recv()
        bit = (my_ctx >> stage) & 1
        merged = []
        for t in range(n_ctx >> (stage + 1)):
            value, top, weight = chunk(head, stage, 2 * t + bit)
            span = slice(t * ctx_rows, (t + 1) * ctx_rows)
            other = sum_recv[stage][head, :, span].astype(jnp.float32)
            other_top = stat_recv[stage][head, 0:1, span]
            other_weight = stat_recv[stage][head, 1:2, span]
            highest = jnp.maximum(top, other_top)
            mine = jnp.exp2(top - highest)
            theirs = jnp.exp2(other_top - highest)
            merged.append((
                value * mine + other * theirs,
                highest,
                weight * mine + other_weight * theirs,
            ))
            if stage + 1 < n_stage:
                acc[head, :, span], high[head, :, span], total[head, :, span] = merged[-1]
        return merged[0]

    def send_out(head, value, weight):
        attended = (value / weight).astype(jnp.bfloat16)
        for piece in range(n_head):
            head_out[piece, head] = attended[:, piece * own_rows:(piece + 1) * own_rows]
        for mask in range(1, n_head):
            copy = pltpu.make_async_remote_copy(
                src_ref=head_out.at[my_head ^ mask, head],
                dst_ref=head_in.at[my_head, head],
                send_sem=out_ssem.at[mask - 1, head],
                recv_sem=out_rsem.at[mask - 1, head],
                device_id={"head": my_head ^ mask},
                device_id_type=MESH,
            )
            copy.start()
            copies.append(copy)
            pending["out", head, mask] = copy
        head_in[my_head, head] = head_out[my_head, head]

    def advance(head, stage):
        merged = merge_stage(head, stage)
        if stage + 1 < n_stage:
            send_stage(head, stage + 1)
        else:
            send_out(head, merged[0], merged[2])

    for step in range(heads_local + n_stage):
        if step < heads_local:
            if step % 2 == 0:
                advance_w()
            for mask in far:
                kv_copies[mask, step].wait_recv()
                attend(mask, step, False)
            send_stage(step, 0)
        for stage in range(n_stage):
            head = step - 1 - stage
            if 0 <= head < heads_local:
                advance(head, stage)

    while w_done[0] <= len(w_steps):
        advance_w()
    for head in range(heads_local):
        for mask in range(1, n_head):
            pending["out", head, mask].wait_recv()
    joined = head_in[...].astype(jnp.float32).reshape(
        n_head * heads_local * head_size, own_rows
    )
    mean_square = jnp.sum(joined * joined, axis=0, keepdims=True) / joined.shape[0]
    normed = (joined * gain_ref[...] * lax.rsqrt(mean_square + epsilon)).astype(jnp.bfloat16)
    rows = normed.T
    for mask in range(n_part):
        weights = w_all[mask].reshape(joined.shape[0], part_width)
        target = pl.ds(pl.multiple_of((my_part ^ mask) * part_width, part_width), part_width)
        out_ref[:, target] = jnp.dot(
            rows, weights, preferred_element_type=jnp.float32
        ).astype(jnp.bfloat16)

    for copy in list(kv_copies.values()) + weight_copies + copies:
        copy.wait_send()


def body(context, w_kv, queries, gain, w_out):
    heads_local, head_size, latents = queries.shape
    model_width = w_kv.shape[0]
    n_head = lax.axis_size("head")
    n_ctx = lax.axis_size("ctx")
    n_stage = n_ctx.bit_length() - 1
    rows = context.shape[0]
    ctx_rows = latents // n_ctx
    own_rows = ctx_rows // n_head
    n_part = min(lax.axis_size("groups") * n_ctx, model_width // 128)

    def stage_buffers(depth, kind):
        return [
            pltpu.VMEM((heads_local, depth, (n_ctx >> (s + 1)) * ctx_rows), kind)
            for s in range(n_stage)
        ]

    dma = pltpu.SemaphoreType.DMA
    vmem = pl.BlockSpec(memory_space=pltpu.VMEM)
    return pl.pallas_call(
        functools.partial(attention_kernel, n_head, n_ctx, n_part, min(1024, latents)),
        out_shape=jax.ShapeDtypeStruct((own_rows, model_width), jnp.bfloat16),
        in_specs=[vmem] * 5,
        out_specs=vmem,
        scratch_shapes=[
            pltpu.VMEM((n_head - 1, heads_local, rows, 2 * head_size), jnp.bfloat16),
            pltpu.VMEM((n_head, heads_local, rows, 2 * head_size), jnp.bfloat16),
            pltpu.VMEM((heads_local, head_size, latents), jnp.float32),
            pltpu.VMEM((heads_local, 1, latents), jnp.float32),
            pltpu.VMEM((heads_local, 1, latents), jnp.float32),
            pltpu.VMEM((n_head, heads_local, head_size, own_rows), jnp.bfloat16),
            pltpu.VMEM((n_head, heads_local, head_size, own_rows), jnp.bfloat16),
            pltpu.VMEM(
                (n_part, n_head, w_out.shape[0], model_width // n_part), jnp.bfloat16
            ),
            *stage_buffers(head_size, jnp.bfloat16),
            *stage_buffers(head_size, jnp.bfloat16),
            *stage_buffers(2, jnp.float32),
            *stage_buffers(2, jnp.float32),
            dma((n_head - 1, heads_local)),
            dma((n_head - 1, heads_local)),
            dma((n_stage, heads_local)),
            dma((n_stage, heads_local)),
            dma((n_stage, heads_local)),
            dma((n_stage, heads_local)),
            dma((n_head - 1, heads_local)),
            dma((n_head - 1, heads_local)),
            dma((n_head - 1,)),
            dma((n_head - 1,)),
            dma((n_part - 1,)),
            dma((n_part - 1,)),
        ],
        compiler_params=pltpu.CompilerParams(
            collective_id=0, has_side_effects=True, vmem_limit_bytes=48 * 1024 * 1024
        ),
        cost_estimate=pl.CostEstimate(
            flops=4 * heads_local * latents * rows * n_head * head_size
            + 4 * rows * model_width * model_width,
            bytes_accessed=2 * w_kv.size + 2 * context.size + 2 * queries.size,
            transcendentals=heads_local * latents * rows * n_head,
        ),
    )(context, w_kv, queries, gain.reshape(model_width, 1), w_out)


def solution(mesh):
    return jax.shard_map(
        body,
        mesh=mesh,
        in_specs=(
            P(("groups", "ctx", "head"), None),
            P(),
            P(("groups", "head"), None, None),
            P(),
            P("head", None),
        ),
        out_specs=P(("groups", "ctx", "head"), None),
        check_vma=False,
    )
```

```python
import functools
import math

import jax
import jax.numpy as jnp
from jax import lax
from jax.experimental import pallas as pl
from jax.experimental.pallas import tpu as pltpu
from jax.sharding import PartitionSpec as P

epsilon = 1e-06
MESH = pl.DeviceIdType.MESH


def attention_kernel(
    n_head, n_ctx, n_part, q_tile,
    context_ref, w_kv_ref, queries_ref, gain_ref, w_out_ref,
    out_ref,
    kv_send, kv_all, acc, high, total, head_out, head_in, w_all, *rest,
):
    n_stage = n_ctx.bit_length() - 1
    sum_send, rest = rest[:n_stage], rest[n_stage:]
    sum_recv, rest = rest[:n_stage], rest[n_stage:]
    stat_send, rest = rest[:n_stage], rest[n_stage:]
    stat_recv, rest = rest[:n_stage], rest[n_stage:]
    kv_ssem, kv_rsem, sum_ssem, sum_rsem, stat_ssem, stat_rsem, out_ssem, out_rsem = rest[:8]
    wh_ssem, wh_rsem, wp_ssem, wp_rsem = rest[8:]

    heads_local, head_size, latents = queries_ref.shape
    width = 2 * head_size
    group_width = heads_local * width
    ctx_rows = latents // n_ctx
    own_rows = ctx_rows // n_head
    scale = math.log2(math.e) / math.sqrt(head_size)
    my_head = lax.axis_index("head")
    my_ctx = lax.axis_index("ctx")
    my_group = lax.axis_index("groups")
    ctx_parts = min(n_ctx, n_part)
    group_bits = (n_part // ctx_parts).bit_length() - 1
    my_part = (my_group & ((1 << group_bits) - 1)) * ctx_parts + (my_ctx & (ctx_parts - 1))
    part_width = w_all.shape[3]

    barrier = pltpu.get_barrier_semaphore()
    for mask in range(1, n_head):
        pl.semaphore_signal(
            barrier, inc=1, device_id={"head": my_head ^ mask}, device_id_type=MESH
        )
    for stage in range(n_stage):
        pl.semaphore_signal(
            barrier, inc=1, device_id={"ctx": my_ctx ^ (1 << stage)}, device_id_type=MESH
        )
    for level in range(group_bits):
        pl.semaphore_signal(
            barrier, inc=1, device_id={"groups": my_group ^ (1 << level)}, device_id_type=MESH
        )
    part_span = pl.ds(pl.multiple_of(my_part * part_width, part_width), part_width)
    w_all[0, my_head] = w_out_ref[:, part_span]

    def project(target):
        columns = pl.ds(pl.multiple_of(target * group_width, group_width), group_width)
        return jnp.dot(
            context_ref[...], w_kv_ref[:, columns], preferred_element_type=jnp.float32
        ).astype(jnp.bfloat16)

    weight_copies = []
    w_pending = {}

    def send_w(key, source, target, ssem, rsem, where):
        copy = pltpu.make_async_remote_copy(
            src_ref=source,
            dst_ref=target,
            send_sem=ssem,
            recv_sem=rsem,
            device_id=where,
            device_id_type=MESH,
        )
        copy.start()
        weight_copies.append(copy)
        w_pending.setdefault(key, []).append(copy)

    def receive_w(key):
        for copy in w_pending[key]:
            copy.wait_recv()

    part_levels = list(reversed(range(n_part.bit_length() - 1)))
    part_masks = [0]

    def w_head(level):
        for mask in range(n_head - 1, 0, -1):
            block = w_all.at[0, my_head]
            send_w(
                ("head", level), block, block,
                wh_ssem.at[mask - 1], wh_rsem.at[mask - 1], {"head": my_head ^ mask},
            )

    def w_part(level):
        bit = 1 << level
        if bit >= ctx_parts:
            where = {"groups": my_group ^ (bit // ctx_parts)}
        else:
            where = {"ctx": my_ctx ^ bit}
        for mask in part_masks:
            index = (mask | bit) - 1
            send_w(
                ("part", level), w_all.at[mask], w_all.at[mask | bit],
                wp_ssem.at[index], wp_rsem.at[index], where,
            )
        part_masks.extend([mask | bit for mask in part_masks])

    w_steps = [("head", 0)]
    w_steps += [("part", level) for level in part_levels]
    w_done = [0]

    def advance_w():
        index = w_done[0]
        if index > len(w_steps):
            return
        if index:
            receive_w(w_steps[index - 1])
        if index < len(w_steps):
            kind, level = w_steps[index]
            (w_head if kind == "head" else w_part)(level)
        w_done[0] = index + 1

    near = [1] if n_head > 1 else []
    far = list(range(n_head - 1, 1, -1))
    kv_copies = {}

    def send_kv(mask, head):
        kv_copies[mask, head] = pltpu.make_async_remote_copy(
            src_ref=kv_send.at[mask - 1, head],
            dst_ref=kv_all.at[mask, head],
            send_sem=kv_ssem.at[mask - 1, head],
            recv_sem=kv_rsem.at[mask - 1, head],
            device_id={"head": my_head ^ mask},
            device_id_type=MESH,
        )
        kv_copies[mask, head].start()

    def project_into(mask, target):
        projected = project(my_head ^ mask)
        for head in range(heads_local):
            target[mask - 1 if mask else 0, head] = projected[:, head * width:(head + 1) * width]

    for mask in far + near:
        project_into(mask, kv_send)
        if mask == (far + near)[0]:
            pl.semaphore_wait(barrier, n_head - 1 + n_stage + group_bits)
            advance_w()
        if len(far) > 1 and mask == far[0]:
            send_kv(mask, 0)
        elif far and mask == far[-1]:
            send_kv(mask, 0)
        elif mask == 1:
            for head in range(heads_local):
                for other in far + near:
                    if (other, head) not in kv_copies:
                        send_kv(other, head)
    project_into(0, kv_all)

    def attend(slot, head, first):
        block = kv_all[slot, head]
        key = block[:, :head_size]
        value = block.T[head_size:, :]
        for tile in range(latents // q_tile):
            span = slice(tile * q_tile, (tile + 1) * q_tile)
            scores = (
                jnp.dot(key, queries_ref[head, :, span], preferred_element_type=jnp.float32)
                * scale
            )
            highest = jnp.max(scores, axis=0, keepdims=True)
            if not first:
                before = high[head, :, span]
                highest = jnp.maximum(highest, before)
                factor = jnp.exp2(before - highest)
            weights = jnp.exp2(scores - highest)
            row_total = jnp.sum(weights, axis=0, keepdims=True)
            summed = jnp.dot(
                value, weights.astype(jnp.bfloat16), preferred_element_type=jnp.float32
            )
            if not first:
                row_total += total[head, :, span] * factor
                summed += acc[head, :, span] * factor
            high[head, :, span] = highest
            total[head, :, span] = row_total
            acc[head, :, span] = summed

    def one_head(head, carry):
        attend(0, head, True)
        return carry

    lax.fori_loop(0, heads_local, one_head, 0)
    advance_w()

    copies = []
    pending = {}
    held = {}

    def chunk(head, stage, index):
        if stage == 0:
            span = pl.ds(pl.multiple_of(index * ctx_rows, ctx_rows), ctx_rows)
            return acc[head, :, span], high[head, :, span], total[head, :, span]
        source = pl.ds(pl.multiple_of(index * ctx_rows, ctx_rows), ctx_rows)
        return acc[head, :, source], high[head, :, source], total[head, :, source]

    def send_stage(head, stage):
        bit = (my_ctx >> stage) & 1
        for t in range(n_ctx >> (stage + 1)):
            value, top, weight = chunk(head, stage, 2 * t + 1 - bit)
            span = slice(t * ctx_rows, (t + 1) * ctx_rows)
            sum_send[stage][head, :, span] = value.astype(jnp.bfloat16)
            stat_send[stage][head, 0:1, span] = top
            stat_send[stage][head, 1:2, span] = weight
        pair = []
        for source, target, ssem, rsem in (
            (sum_send, sum_recv, sum_ssem, sum_rsem),
            (stat_send, stat_recv, stat_ssem, stat_rsem),
        ):
            copy = pltpu.make_async_remote_copy(
                src_ref=source[stage].at[head],
                dst_ref=target[stage].at[head],
                send_sem=ssem.at[stage, head],
                recv_sem=rsem.at[stage, head],
                device_id={"ctx": my_ctx ^ (1 << stage)},
                device_id_type=MESH,
            )
            copy.start()
            pair.append(copy)
        copies.extend(pair)
        pending[head, stage] = pair

    def merge_stage(head, stage):
        for copy in pending[head, stage]:
            copy.wait_recv()
        bit = (my_ctx >> stage) & 1
        merged = []
        for t in range(n_ctx >> (stage + 1)):
            value, top, weight = chunk(head, stage, 2 * t + bit)
            span = slice(t * ctx_rows, (t + 1) * ctx_rows)
            other = sum_recv[stage][head, :, span].astype(jnp.float32)
            other_top = stat_recv[stage][head, 0:1, span]
            other_weight = stat_recv[stage][head, 1:2, span]
            highest = jnp.maximum(top, other_top)
            mine = jnp.exp2(top - highest)
            theirs = jnp.exp2(other_top - highest)
            merged.append((
                value * mine + other * theirs,
                highest,
                weight * mine + other_weight * theirs,
            ))
            if stage + 1 < n_stage:
                acc[head, :, span], high[head, :, span], total[head, :, span] = merged[-1]
        return merged[0]

    def send_out(head, value, weight):
        attended = (value / weight).astype(jnp.bfloat16)
        for piece in range(n_head):
            head_out[piece, head] = attended[:, piece * own_rows:(piece + 1) * own_rows]
        for mask in range(1, n_head):
            copy = pltpu.make_async_remote_copy(
                src_ref=head_out.at[my_head ^ mask, head],
                dst_ref=head_in.at[my_head, head],
                send_sem=out_ssem.at[mask - 1, head],
                recv_sem=out_rsem.at[mask - 1, head],
                device_id={"head": my_head ^ mask},
                device_id_type=MESH,
            )
            copy.start()
            copies.append(copy)
            pending["out", head, mask] = copy
        head_in[my_head, head] = head_out[my_head, head]

    def advance(head, stage):
        merged = merge_stage(head, stage)
        if stage + 1 < n_stage:
            send_stage(head, stage + 1)
        else:
            send_out(head, merged[0], merged[2])

    for step in range(heads_local + n_stage):
        if step < heads_local:
            if step:
                advance_w()
            for mask in near + far:
                kv_copies[mask, step].wait_recv()
                attend(mask, step, False)
            send_stage(step, 0)
        for stage in range(n_stage):
            head = step - 1 - stage
            if 0 <= head < heads_local:
                advance(head, stage)

    while w_done[0] <= len(w_steps):
        advance_w()
    for head in range(heads_local):
        for mask in range(1, n_head):
            pending["out", head, mask].wait_recv()
    joined = head_in[...].astype(jnp.float32).reshape(
        n_head * heads_local * head_size, own_rows
    )
    mean_square = jnp.sum(joined * joined, axis=0, keepdims=True) / joined.shape[0]
    normed = (joined * gain_ref[...] * lax.rsqrt(mean_square + epsilon)).astype(jnp.bfloat16)
    rows = normed.T
    for mask in range(n_part):
        weights = w_all[mask].reshape(joined.shape[0], part_width)
        target = pl.ds(pl.multiple_of((my_part ^ mask) * part_width, part_width), part_width)
        out_ref[:, target] = jnp.dot(
            rows, weights, preferred_element_type=jnp.float32
        ).astype(jnp.bfloat16)

    for copy in list(kv_copies.values()) + weight_copies + copies:
        copy.wait_send()


def body(context, w_kv, queries, gain, w_out):
    heads_local, head_size, latents = queries.shape
    model_width = w_kv.shape[0]
    n_head = lax.axis_size("head")
    n_ctx = lax.axis_size("ctx")
    n_stage = n_ctx.bit_length() - 1
    rows = context.shape[0]
    ctx_rows = latents // n_ctx
    own_rows = ctx_rows // n_head
    n_part = min(lax.axis_size("groups") * n_ctx, model_width // 128)

    def stage_buffers(depth, kind):
        return [
            pltpu.VMEM((heads_local, depth, (n_ctx >> (s + 1)) * ctx_rows), kind)
            for s in range(n_stage)
        ]

    dma = pltpu.SemaphoreType.DMA
    vmem = pl.BlockSpec(memory_space=pltpu.VMEM)
    return pl.pallas_call(
        functools.partial(attention_kernel, n_head, n_ctx, n_part, min(2048, latents)),
        out_shape=jax.ShapeDtypeStruct((own_rows, model_width), jnp.bfloat16),
        in_specs=[vmem] * 5,
        out_specs=vmem,
        scratch_shapes=[
            pltpu.VMEM((n_head - 1, heads_local, rows, 2 * head_size), jnp.bfloat16),
            pltpu.VMEM((n_head, heads_local, rows, 2 * head_size), jnp.bfloat16),
            pltpu.VMEM((heads_local, head_size, latents), jnp.float32),
            pltpu.VMEM((heads_local, 1, latents), jnp.float32),
            pltpu.VMEM((heads_local, 1, latents), jnp.float32),
            pltpu.VMEM((n_head, heads_local, head_size, own_rows), jnp.bfloat16),
            pltpu.VMEM((n_head, heads_local, head_size, own_rows), jnp.bfloat16),
            pltpu.VMEM(
                (n_part, n_head, w_out.shape[0], model_width // n_part), jnp.bfloat16
            ),
            *stage_buffers(head_size, jnp.bfloat16),
            *stage_buffers(head_size, jnp.bfloat16),
            *stage_buffers(2, jnp.float32),
            *stage_buffers(2, jnp.float32),
            dma((n_head - 1, heads_local)),
            dma((n_head - 1, heads_local)),
            dma((n_stage, heads_local)),
            dma((n_stage, heads_local)),
            dma((n_stage, heads_local)),
            dma((n_stage, heads_local)),
            dma((n_head - 1, heads_local)),
            dma((n_head - 1, heads_local)),
            dma((n_head - 1,)),
            dma((n_head - 1,)),
            dma((n_part - 1,)),
            dma((n_part - 1,)),
        ],
        compiler_params=pltpu.CompilerParams(
            collective_id=0, has_side_effects=True, vmem_limit_bytes=48 * 1024 * 1024
        ),
        cost_estimate=pl.CostEstimate(
            flops=4 * heads_local * latents * rows * n_head * head_size
            + 4 * rows * model_width * model_width,
            bytes_accessed=2 * w_kv.size + 2 * context.size + 2 * queries.size,
            transcendentals=heads_local * latents * rows * n_head,
        ),
    )(context, w_kv, queries, gain.reshape(model_width, 1), w_out)


def solution(mesh):
    return jax.shard_map(
        body,
        mesh=mesh,
        in_specs=(
            P(("groups", "ctx", "head"), None),
            P(),
            P(("groups", "head"), None, None),
            P(),
            P("head", None),
        ),
        out_specs=P(("groups", "ctx", "head"), None),
        check_vma=False,
    )
```
